128 devices in a mesh: lat: 16 (over y, x_hi, core), lon: 8 (over x_lo, z).
Axes of the slice: x: 4 (x_hi: 2, x_lo: 2; x = x_hi * 2 + x_lo), y: 4, z: 4, core: 2. Of those that a mesh axis runs over, the one named last changes fastest.
Arguments:
- fine: bfloat16 [256, 1024, 384], P('lat', 'lon'), may hold values from -6 to 6
- conv_weight: bfloat16 [3, 3, 384, 384], replicated, may hold values from -0.109375 to 0.109375
- merge_weight: bfloat16 [1536, 1024], replicated, may hold values from -0.15625 to 0.15625
- qkv_weight: bfloat16 [1024, 3072], replicated, may hold values from -0.1875 to 0.1875
- proj_weight: bfloat16 [1024, 1024], replicated, may hold values from -0.1875 to 0.1875
- up_weight: bfloat16 [1024, 1536], replicated, may hold values from -0.1875 to 0.1875
- logit_scale: float32 [16], replicated, may hold values from 3 to 100
- pos_bias: float32 [16, 225], replicated, may hold values from -4 to 4
- shift: int32 [2], replicated, may hold values from 1 to 7
Outputs:
- result: bfloat16 [256, 1024, 384], P('lat', 'lon')
The draws below stay inside these ranges and needn't reach their ends.
All inputs are finite; a program needn't handle non-finite values.
Results may differ from the reference program's by a relative error of at most 0.03.
Values may be sent and summed in bfloat16 or wider, within the bound.
No kernel may reach another device: no remote copies, remote signals or barrier semaphores. Data moves between devices by JAX's collectives and lax.ppermute only.
A program may use at most 128 MiB of HBM per device.

```python
import jax
import jax.numpy as jnp
from jax import lax

CF = 384
CM = 1024
HEADS = 16
WIN = 8
FR = 256
FC = 1024


def draw_logit_scale(key, part):
    key = jax.random.fold_in(key, 11)
    key_level, key_top = jax.random.split(key)
    level = jax.random.uniform(key_level, (HEADS,), jnp.float32, 0.0, 1.0)
    values = 3.0 * jnp.exp(level * jnp.log(100.0 / 3.0))
    top_head = jax.random.randint(key_top, (), 0, HEADS)
    values = jnp.where(jnp.arange(HEADS) == top_head, 100.0, values)
    return jnp.clip(values, 3.0, 100.0).astype(jnp.float32)


def draw_qkv_weight(key, part):
    key = jax.random.fold_in(key, 23)
    entries = jax.random.normal(key, (CM, 3 * CM), jnp.float32)
    entries = jnp.clip(entries, -6.0, 6.0) * CM ** (-0.5)
    return entries.astype(jnp.bfloat16)


def block_scale(stream_key, dims, shards, least, top_value):
    def one(axis_at, shards_of):
        draws = jax.random.uniform(jax.random.fold_in(jax.random.fold_in(stream_key, 6), axis_at), (shards_of,), jnp.float32, least / len(shards), top_value / len(shards))
        return jnp.repeat(jnp.exp(draws), dims[axis_at] // shards_of).reshape((-1,) + (1,) * (len(dims) - axis_at - 1))

    gain = one(*shards[0])
    for cut in shards[1:]:
        gain = gain * one(*cut)
    return gain


def gaussian(stream_key, extent, width, most, shards=(), kind=jnp.bfloat16):
    result = jax.random.normal(stream_key, extent, jnp.float32) * width
    if len(shards) > 0:
        result = block_scale(stream_key, extent, shards, -0.22, 0.18) * result
    return jnp.clip(result, min=-most, max=most).astype(kind)


def setup_inputs(seed: int = 0) -> dict:
    splits = jax.random.split(jax.random.key(seed), 10)
    return {
        "fine": gaussian(splits[0], (FR, FC, CF), 1.0, 6.0, ((0, 16), (1, 8))),
        "conv_weight": gaussian(splits[1], (3, 3, CF, CF), (9 * CF) ** -0.5, 0.109375),
        "merge_weight": gaussian(splits[2], (4 * CF, CM), (4 * CF) ** -0.5, 0.15625),
        "qkv_weight": draw_qkv_weight(jax.random.fold_in(splits[9], 71), 0),
        "proj_weight": gaussian(splits[4], (CM, CM), CM ** -0.5, 0.1875),
        "up_weight": gaussian(splits[5], (CM, 4 * CF), CM ** -0.5, 0.1875),
        "logit_scale": draw_logit_scale(jax.random.fold_in(splits[9], 71), 0),
        "pos_bias": gaussian(splits[7], (HEADS, (2 * WIN - 1) * (2 * WIN - 1)), 1.0, 4.0, (), jnp.float32),
        "shift": jax.random.randint(splits[8], (2,), 1, WIN).astype(jnp.int32),
    }


EPS = 1e-05
QK_EPS = 1e-06
MASKED = -1e+30

def normalize(values):
    values = values.astype(jnp.float32)
    center = values - lax.optimization_barrier(jnp.mean(values, axis=-1, keepdims=True))
    return center * lax.rsqrt(lax.optimization_barrier(jnp.mean(center * center, axis=-1, keepdims=True)) + EPS)

def relative_index(window):
    position = jnp.arange(window * window)
    pos_row = position // window
    pos_col = position % window
    return (pos_row[:, None] - pos_row[None, :] + window - 1) * (2 * window - 1) + (pos_col[:, None] - pos_col[None, :] + window - 1)

def project_heads(tokens, qkv_weight, heads):
    token_count, width_model = tokens.shape
    head_dim = width_model // heads
    projected = jnp.dot(normalize(tokens).astype(jnp.bfloat16), qkv_weight, preferred_element_type=jnp.float32)
    query_part = projected[:, :width_model].reshape(token_count, heads, head_dim)
    key_part = projected[:, width_model:2 * width_model].reshape(token_count, heads, head_dim)
    value_part = projected[:, 2 * width_model:]
    query_part = query_part * lax.rsqrt(lax.optimization_barrier(jnp.sum(query_part * query_part, -1, keepdims=True)) + QK_EPS)
    key_part = key_part * lax.rsqrt(lax.optimization_barrier(jnp.sum(key_part * key_part, -1, keepdims=True)) + QK_EPS)
    return jnp.concatenate([query_part.reshape(token_count, width_model), key_part.reshape(token_count, width_model), value_part], 1).astype(jnp.bfloat16)

def attend_windows(packed, region, logit_scale, bias):
    heads = logit_scale.shape[0]
    n_win, span, triple = packed.shape
    width_model = triple // 3
    head_dim = width_model // heads
    parts = packed.astype(jnp.float32).reshape(n_win, span, 3, heads, head_dim)
    scores = jnp.einsum('nahd,nbhd->nhab', parts[:, :, 0], parts[:, :, 1])
    scores = scores * logit_scale[None, :, None, None] + bias[None]
    allowed = region[:, :, None] == region[:, None, :]
    scores = jnp.where(allowed[:, None], scores, MASKED)
    weights = jnp.exp(scores - lax.optimization_barrier(jnp.max(scores, -1, keepdims=True)))
    probs = (weights / lax.optimization_barrier(jnp.sum(weights, -1, keepdims=True))).astype(jnp.bfloat16)
    output = jnp.einsum('nhab,nbhd->nahd', probs.astype(jnp.float32), parts[:, :, 2])
    return output.reshape(n_win, span, width_model).astype(jnp.bfloat16)

def merge_tokens(layout, merge_weight):
    row_count, col_count, chan_count = layout.shape
    blocks = layout.reshape(row_count // 2, 2, col_count // 2, 2, chan_count).transpose(0, 2, 3, 1, 4)
    blocks = blocks.reshape(row_count // 2 * (col_count // 2), 4 * chan_count)
    merged = jnp.dot(normalize(blocks).astype(jnp.bfloat16), merge_weight, preferred_element_type=jnp.float32)
    return merged.astype(jnp.bfloat16).reshape(row_count // 2, col_count // 2, -1)

def split_tokens(restored, up_weight, conv_out):
    row_count, col_count, width_model = restored.shape
    chan_count = conv_out.shape[-1]
    spread = jnp.dot(restored.reshape(-1, width_model), up_weight, preferred_element_type=jnp.float32)
    spread = spread.reshape(row_count, col_count, 2, 2, chan_count).transpose(0, 3, 1, 2, 4)
    spread = spread.reshape(2 * row_count, 2 * col_count, chan_count)
    return (conv_out.astype(jnp.float32) + spread).astype(jnp.bfloat16)

def reference(fine, conv_weight, merge_weight, qkv_weight, proj_weight, up_weight, logit_scale, pos_bias, shift):
    fine_rows, fine_cols, chan_count = fine.shape
    activated = jax.nn.silu(normalize(fine)).astype(jnp.bfloat16)
    padded = jnp.pad(activated, ((1, 1), (0, 0), (0, 0)))
    running = jnp.zeros((fine_rows * fine_cols, chan_count), jnp.float32)
    for row_tap in range(3):
        band_rows = padded[row_tap:row_tap + fine_rows]
        for col_tap in range(3):
            moved = jnp.roll(band_rows, 1 - col_tap, axis=1).reshape(-1, chan_count)
            running = running + jnp.dot(moved, conv_weight[row_tap, col_tap], preferred_element_type=jnp.float32)
    conv_out = (fine.reshape(-1, chan_count).astype(jnp.float32) + running).astype(jnp.bfloat16).reshape(fine.shape)
    coarse = merge_tokens(conv_out, merge_weight)
    coarse_rows, coarse_cols, width_model = coarse.shape
    heads = logit_scale.shape[0]
    row_shift = shift[0]
    col_shift = shift[1]
    rolled = jnp.roll(coarse, (-row_shift, -col_shift), axis=(0, 1))
    packed = project_heads(rolled.reshape(-1, width_model), qkv_weight, heads).reshape(coarse_rows, coarse_cols, 3 * width_model)
    region = jnp.broadcast_to((jnp.arange(coarse_rows) >= coarse_rows - row_shift)[:, None], (coarse_rows, coarse_cols))
    bias = pos_bias[:, relative_index(WIN)]
    win_rows = coarse_rows // WIN
    win_cols = coarse_cols // WIN
    tiles = packed.reshape(win_rows, WIN, win_cols, WIN, 3 * width_model).transpose(0, 2, 1, 3, 4)
    tiles = tiles.reshape(win_rows, win_cols, WIN * WIN, 3 * width_model)
    marks = region.reshape(win_rows, WIN, win_cols, WIN).transpose(0, 2, 1, 3).reshape(win_rows, win_cols, WIN * WIN)
    attended = lax.map(lambda pair: attend_windows(pair[0], pair[1], logit_scale, bias), (tiles, marks))
    attended = attended.reshape(win_rows, win_cols, WIN, WIN, width_model).transpose(0, 2, 1, 3, 4)
    attended = attended.reshape(coarse_rows * coarse_cols, width_model)
    mixed = rolled.reshape(-1, width_model).astype(jnp.float32) + jnp.dot(attended, proj_weight, preferred_element_type=jnp.float32)
    mixed = mixed.astype(jnp.bfloat16).reshape(coarse_rows, coarse_cols, width_model)
    restored = jnp.roll(mixed, (row_shift, col_shift), axis=(0, 1))
    return split_tokens(restored, up_weight, conv_out)
```

```python
import jax
import jax.numpy as jnp
from jax import lax
from jax.sharding import PartitionSpec as P
from jax.experimental import pallas as pl
from jax.experimental.pallas import tpu as pltpu
bf=jnp.bfloat16; f32=jnp.float32
EPS=1e-5; QK_EPS=1e-6; MASKED=-1e30
WIN=8

def norm(x):
    c = x - jnp.mean(x, axis=-1, keepdims=True)
    return c * lax.rsqrt(jnp.mean(c*c, axis=-1, keepdims=True) + EPS)

def act_fn(x):
    n = norm(x.astype(f32))
    return n / (1.0 + jnp.exp(-n))

def k1_body(scal, fine_h, top, bot, left, right, cw_h, mw_h, conv_out, coarse,
            fine, cw, mw, rowbuf, sides, act4, nb, sem):
    cfine = pltpu.make_async_copy(fine_h, fine, sem.at[0]); cfine.start()
    ccw = pltpu.make_async_copy(cw_h, cw, sem.at[1]); ccw.start()
    cmw = pltpu.make_async_copy(mw_h, mw, sem.at[2]); cmw.start()
    top_on = scal[2] > 0
    bot_on = scal[2] < 15
    sides[0] = act_fn(left[...])
    sides[1] = act_fn(right[...])
    def put(r, a):
        lo = sides[0, pl.ds(r, 1)]; hi = sides[1, pl.ds(r, 1)]
        for m in range(3):
            rowbuf[m, 8:136] = a[:, m*128:m*128+128]
            rowbuf[m, 7:8] = lo[:, m*128:m*128+128]
            rowbuf[m, 136:137] = hi[:, m*128:m*128+128]
        act4[r] = jnp.concatenate([rowbuf[m, pl.ds(7 + k, 64, stride=2)] for k in range(4) for m in range(3)], axis=1).astype(bf)
    put(0, act_fn(top[0]))
    put(17, act_fn(bot[0]))
    @pl.when(jnp.logical_not(top_on))
    def _():
        act4[0] = jnp.zeros((64, 1536), bf)
    @pl.when(jnp.logical_not(bot_on))
    def _():
        act4[17] = jnp.zeros((64, 1536), bf)
    cfine.wait()
    @pl.loop(0, 16)
    def _(r):
        put(r + 1, act_fn(fine[r]))
    ccw.wait()
    @pl.loop(0, 4)
    def _(g):
        g4 = g * 4
        lhs = []
        for q in range(2):
            lhs.append(jnp.concatenate(
                [act4[pl.ds(g4 + a, 4), :, q*384:q*384+1152].reshape(256, 1152) for a in range(3)], axis=1))
        out = jnp.dot(jnp.concatenate(lhs, axis=0), cw[...], preferred_element_type=f32)
        for t in range(4):
            row = fine[g4 + t].astype(f32)
            for m in range(3):
                rowbuf[m, 0:128] = row[:, m*128:m*128+128]
            for q in range(2):
                o = out[q*256 + t*64: q*256 + t*64 + 64] + jnp.concatenate([rowbuf[m, pl.ds(q, 64, stride=2)] for m in range(3)], axis=1)
                conv_out[g4 + t, q] = o.astype(bf)
        for t in range(2):
            blk = jnp.concatenate([conv_out[g4 + 2*t + p, q].astype(f32) for q in range(2) for p in range(2)], axis=1)
            nb[2*g + t] = norm(blk).astype(bf)
    cmw.wait()
    @pl.loop(0, 4)
    def _(n):
        sl = pl.ds(pl.multiple_of(n*256, 256), 256)
        coarse[:, :, sl] = jnp.dot(nb[...].reshape(512, 1536), mw[:, sl], preferred_element_type=f32).astype(bf).reshape(8, 64, 256)

VM = pl.BlockSpec(memory_space=pltpu.VMEM); AN = pl.BlockSpec(memory_space=pl.ANY); SM = pl.BlockSpec(memory_space=pltpu.SMEM)

def k1(scal, fine, top, bot, left, right, cw, mw):
    return pl.pallas_call(
        k1_body,
        out_shape=[jax.ShapeDtypeStruct((16, 2, 64, 384), bf), jax.ShapeDtypeStruct((8, 64, 1024), bf)],
        in_specs=[SM, AN, VM, VM, VM, VM, AN, AN],
        out_specs=[VM, VM],
        scratch_shapes=[pltpu.VMEM((16,128,384), bf), pltpu.VMEM((3456,384), bf), pltpu.VMEM((1536,1024), bf),
            pltpu.VMEM((3,144,128), f32), pltpu.VMEM((2,18,384), f32), pltpu.VMEM((18,64,1536), bf), pltpu.VMEM((8,64,1536), bf),
            pltpu.SemaphoreType.DMA((3,))],
        compiler_params=pltpu.CompilerParams(vmem_limit_bytes=48<<20),
        cost_estimate=pl.CostEstimate(flops=7_000_000_000, bytes_accessed=11_000_000, transcendentals=1_000_000),
        name="conv_merge",
    )(scal, fine, top, bot, left, right, cw, mw)

def k2_body(scal, own, rows, right, diag, bias_h, scale, qw_h, pw_h, mixed,
            ext, xr, xn, qkv, att, bias, ones, qw, pw, sem):
    cq = pltpu.make_async_copy(qw_h, qw, sem.at[0]); cq.start()
    cp = pltpu.make_async_copy(pw_h, pw, sem.at[1]); cp.start()
    cb = pltpu.make_async_copy(bias_h, bias, sem.at[2]); cb.start()
    s = scal[0]; c = scal[1]; lat = scal[2]
    up = s <= 4
    o_at = jnp.where(up, 0, 4); r_at = jnp.where(up, 8, 0); start = jnp.where(up, s, s - 4)
    ext[pl.ds(o_at, 8), 0:64] = own[...].astype(f32)
    ext[pl.ds(r_at, 4), 0:64] = rows[...].astype(f32)
    ext[pl.ds(o_at, 8), 64:72] = right[...].astype(f32)
    ext[pl.ds(r_at, 4), 64:72] = diag[...].astype(f32)
    hi = lax.broadcasted_iota(jnp.int32, (256, 256), 0) // 64
    hj = lax.broadcasted_iota(jnp.int32, (256, 256), 1) // 64
    ones[...] = jnp.where(hi == hj, 1.0, 0.0).astype(bf)
    @pl.loop(0, 8)
    def _(r):
        x = pltpu.roll(ext[start + r], 72 - c, axis=0)
        for w in range(8):
            xr[w, pl.ds(pl.multiple_of(r * 8, 8), 8)] = x[8*w:8*w+8]
    @pl.loop(0, 8)
    def _(w):
        xn[w] = norm(xr[w]).astype(bf)
    cq.wait()
    X = lambda: xn[...].reshape(512, 1024)
    @pl.loop(0, 8)
    def _(n):
        sl = pl.ds(pl.multiple_of(n*256, 256), 256)
        t = jnp.dot(X(), qw[:, sl], preferred_element_type=f32)
        ss = jnp.dot((t*t).astype(bf), ones[...], preferred_element_type=f32)
        qkv[:, sl] = (t * lax.rsqrt(ss + QK_EPS)).astype(bf)
    @pl.loop(8, 12)
    def _(n):
        sl = pl.ds(pl.multiple_of(n*256, 256), 256)
        qkv[:, sl] = jnp.dot(X(), qw[:, sl], preferred_element_type=f32).astype(bf)
    cb.wait()
    last = jnp.where(up, lat == 15, lat == 0)
    @pl.when(last)
    def _():
        kr = lax.broadcasted_iota(jnp.int32, (64, 128), 0) // 8
        qr = (lax.broadcasted_iota(jnp.int32, (64, 128), 1) % 64) // 8
        ok = (kr >= 8 - s) == (qr >= 8 - s)
        for p in range(8):
            bias[p] = jnp.where(ok, bias[p], MASKED)
    lane = lax.broadcasted_iota(jnp.int32, (64, 128), 1)
    first = lane < 64
    @pl.loop(0, 8)
    def _(w):
        rw = pl.ds(pl.multiple_of(w*64, 64), 64)
        for p in range(8):
            q = qkv[rw, p*128:p*128+128]
            k = qkv[rw, 1024+p*128:1024+p*128+128]
            v = qkv[rw, 2048+p*128:2048+p*128+128]
            z = jnp.zeros_like(q)
            q2 = jnp.concatenate([jnp.where(first, q, z), jnp.where(first, z, q)], axis=0)
            st = lax.dot_general(k, q2, (((1,), (1,)), ((), ())), preferred_element_type=f32)
            st = st * scale[p:p+1] + bias[p]
            e = jnp.exp(st - jnp.max(st, axis=0, keepdims=True))
            pr = (e * (1.0 / jnp.sum(e, axis=0, keepdims=True))).astype(bf)
            o = lax.dot_general(pr, v, (((0,), (0,)), ((), ())), preferred_element_type=f32)
            att[rw, p*128:p*128+128] = jnp.where(first, o[:64], o[64:]).astype(bf)
    cp.wait()
    @pl.loop(0, 4)
    def _(n):
        sl = pl.ds(pl.multiple_of(n*256, 256), 256)
        m = jnp.dot(att[...], pw[:, sl], preferred_element_type=f32) + xr[:, :, sl].reshape(512, 256)
        m = m.reshape(8, 8, 8, 256)
        for r in range(8):
            mixed[r, :, sl] = m[:, r].reshape(64, 256).astype(bf)

def k2(scal, own, rows, right, diag, bias, scale, qw, pw):
    return pl.pallas_call(
        k2_body,
        out_shape=jax.ShapeDtypeStruct((8, 64, 1024), bf),
        in_specs=[SM, VM, VM, VM, VM, AN, VM, AN, AN],
        out_specs=VM,
        scratch_shapes=[pltpu.VMEM((12,72,1024), f32), pltpu.VMEM((8,64,1024), f32), pltpu.VMEM((8,64,1024), bf), pltpu.VMEM((512,3072), bf),
            pltpu.VMEM((512,1024), bf), pltpu.VMEM((8,64,128), f32), pltpu.VMEM((256,256), bf), pltpu.VMEM((1024,3072), bf), pltpu.VMEM((1024,1024), bf),
            pltpu.SemaphoreType.DMA((3,))],
        compiler_params=pltpu.CompilerParams(vmem_limit_bytes=48<<20),
        cost_estimate=pl.CostEstimate(flops=4_500_000_000, bytes_accessed=11_000_000, transcendentals=1_000_000),
        name="window_attention",
    )(scal, own, rows, right, diag, bias, scale, qw, pw)

def k3_body(scal, own, rows, left, diag, conv_out, uw_h, out, ext, xs, rowbuf, uw, sem):
    cu = pltpu.make_async_copy(uw_h, uw, sem.at[0]); cu.start()
    s = scal[0]; c = scal[1]
    up = s <= 4
    o_at = jnp.where(up, 4, 0); r_at = jnp.where(up, 0, 8); start = jnp.where(up, 4 - s, 8 - s)
    ext[pl.ds(o_at, 8), 8:72] = own[...].astype(f32)
    ext[pl.ds(r_at, 4), 8:72] = rows[...].astype(f32)
    ext[pl.ds(o_at, 8), 0:8] = left[...].astype(f32)
    ext[pl.ds(r_at, 4), 0:8] = diag[...].astype(f32)
    for i in range(8):
        xs[i] = pltpu.roll(ext[start + i], 64 + c, axis=0)[:64].astype(bf)
    cu.wait()
    @pl.loop(0, 2)
    def _(g):
        sp = jnp.dot(xs[pl.ds(g*4, 4)].reshape(256, 1024), uw[...], preferred_element_type=f32)
        for i in range(4):
            for p in range(2):
                r = g*8 + 2*i + p
                for q in range(2):
                    b = 2*q + p
                    o = conv_out[r, q].astype(f32) + sp[i*64:i*64+64, b*384:b*384+384]
                    for m in range(3):
                        rowbuf[m, pl.ds(q, 64, stride=2)] = o[:, m*128:m*128+128]
                out[r] = jnp.concatenate([rowbuf[m] for m in range(3)], axis=1).astype(bf)

def k3(scal, own, rows, left, diag, conv_out, uw):
    return pl.pallas_call(
        k3_body,
        out_shape=jax.ShapeDtypeStruct((16, 128, 384), bf),
        in_specs=[SM, VM, VM, VM, VM, VM, AN],
        out_specs=VM,
        scratch_shapes=[pltpu.VMEM((12,72,1024), f32), pltpu.VMEM((8,64,1024), bf), pltpu.VMEM((3,128,128), f32), pltpu.VMEM((1024,1536), bf),
            pltpu.SemaphoreType.DMA((1,))],
        compiler_params=pltpu.CompilerParams(vmem_limit_bytes=48<<20),
        cost_estimate=pl.CostEstimate(flops=1_600_000_000, bytes_accessed=8_000_000, transcendentals=0),
        name="split_tokens",
    )(scal, own, rows, left, diag, conv_out, uw)


def bias_pairs(pos_bias):
    heads, entries = pos_bias.shape
    position = jnp.arange(WIN * WIN)
    row, col = position // WIN, position % WIN
    relative = (row[None, :] - row[:, None] + WIN - 1) * (2 * WIN - 1) + col[None, :] - col[:, None] + WIN - 1
    one_hot = (relative.reshape(-1)[:, None] == jnp.arange(entries)[None, :]).astype(f32)
    looked = jnp.dot(one_hot, pos_bias.T, precision=lax.Precision.HIGHEST)
    looked = looked.reshape(WIN * WIN, WIN * WIN, heads // 2, 2).transpose(2, 0, 3, 1)
    return looked.reshape(heads // 2, WIN * WIN, 2 * WIN * WIN)


def send(value, lat_step, lon_step):
    lats, lons = lax.axis_size("lat"), lax.axis_size("lon")
    pairs = [
        (a * lons + b, ((a + lat_step) % lats) * lons + (b + lon_step) % lons)
        for a in range(lats)
        for b in range(lons)
    ]
    return lax.ppermute(value, ("lat", "lon"), pairs)


def on_device(fine, conv_weight, merge_weight, qkv_weight, proj_weight, up_weight, logit_scale, pos_bias, shift):
    scal = jnp.concatenate([shift, lax.axis_index("lat").astype(jnp.int32)[None]])
    top = send(fine[15:16], 1, 0)
    bot = send(fine[0:1], -1, 0)
    left = jnp.concatenate([
        send(fine[15:16, 127], 1, 1), send(fine[:, 127], 0, 1), send(fine[0:1, 127], -1, 1)], axis=0)
    right = jnp.concatenate([
        send(fine[15:16, 0], 1, -1), send(fine[:, 0], 0, -1), send(fine[0:1, 0], -1, -1)], axis=0)
    bias = bias_pairs(pos_bias)
    scale = jnp.repeat(logit_scale.reshape(8, 2), 64, axis=1)
    conv_out, coarse = k1(scal, fine, top, bot, left, right, conv_weight.reshape(3456, 384), merge_weight)
    up = shift[0] <= 4

    def ahead_up(v):
        return send(v[:4], -1, 0), send(v[:, :8], 0, -1), send(v[:4, :8], -1, -1)

    def ahead_down(v):
        return send(v[4:], 1, 0), send(v[:, :8], 0, -1), send(v[4:, :8], 1, -1)

    def behind_up(v):
        return send(v[4:], 1, 0), send(v[:, 56:], 0, 1), send(v[4:, 56:], 1, 1)

    def behind_down(v):
        return send(v[:4], -1, 0), send(v[:, 56:], 0, 1), send(v[:4, 56:], -1, 1)

    rows, side, diag = lax.cond(up, ahead_up, ahead_down, coarse)
    mixed = k2(scal, coarse, rows, side, diag, bias, scale, qkv_weight, proj_weight)
    rows, side, diag = lax.cond(up, behind_up, behind_down, mixed)
    return k3(scal, mixed, rows, side, diag, conv_out, up_weight)


def solution(mesh):
    return jax.shard_map(
        on_device,
        mesh=mesh,
        in_specs=(P("lat", "lon", None), P(), P(), P(), P(), P(), P(), P(), P()),
        out_specs=P("lat", "lon", None),
        check_vma=False,
    )
```

```python
import functools
import jax, jax.numpy as jnp
from jax import lax
from jax.experimental import pallas as pl
from jax.experimental.pallas import tpu as pltpu
from jax.sharding import PartitionSpec as P

bf = jnp.bfloat16
f32 = jnp.float32
WIN = 8
EPS = 1e-5
QK_EPS = 1e-6
MASKED = -1e30
VM = pl.BlockSpec(memory_space=pltpu.VMEM)
SM = pl.BlockSpec(memory_space=pltpu.SMEM)
NT = (((1,), (1,)), ((), ()))
TN = (((0,), (0,)), ((), ()))
NN = (((1,), (0,)), ((), ()))


def dot(a, b, dims=NN):
    return lax.dot_general(a, b, dims, preferred_element_type=f32)


def norm(x):
    c = x - jnp.mean(x, axis=-1, keepdims=True)
    return c * lax.rsqrt(jnp.mean(c * c, axis=-1, keepdims=True) + EPS)


def silu_norm(x):
    n = norm(x)
    return n / (1.0 + jnp.exp(-n))


def thirds(x):
    return [x[..., m * 128 : m * 128 + 128] for m in range(3)]


def call(body, name, out_shape, scratch, mib, flops, nbytes, args, n_scalar=1, alias=None):
    single = not isinstance(out_shape, (list, tuple))
    return pl.pallas_call(
        body,
        out_shape=out_shape,
        in_specs=[SM] * n_scalar + [VM] * (len(args) - n_scalar),
        out_specs=VM if single else [VM] * len(out_shape),
        scratch_shapes=scratch,
        input_output_aliases=alias or {},
        compiler_params=pltpu.CompilerParams(vmem_limit_bytes=mib << 20),
        cost_estimate=pl.CostEstimate(flops=flops, bytes_accessed=nbytes, transcendentals=0),
        name=name,
    )(*args)


def conv_body(scal, fine, top, bot, cw, conv_out, edge, act4, raw, split, shift):
    zero_row = jnp.zeros((1, 128), f32)
    for slot in range(8):
        for m in range(3):
            shift[slot, 0, m, 7:8] = zero_row
            shift[slot, 1, m, 72:73] = zero_row

    def activate(r, x, slot, keep):
        for m, part in enumerate(thirds(x.astype(f32))):
            split[slot, m] = part
        even, odd = [
            jnp.concatenate([split[slot, m, pl.ds(q, 64, stride=2)] for m in range(3)], axis=1) for q in range(2)
        ]
        if keep:
            raw[r - 1, 0] = even.astype(bf)
            raw[r - 1, 1] = odd.astype(bf)
        even, odd = silu_norm(even), silu_norm(odd)
        for m in range(3):
            shift[slot, 0, m, 8:72] = odd[:, m * 128 : m * 128 + 128]
            shift[slot, 1, m, 8:72] = even[:, m * 128 : m * 128 + 128]
        before = jnp.concatenate([shift[slot, 0, m, 7:71] for m in range(3)], axis=1)
        after = jnp.concatenate([shift[slot, 1, m, 9:73] for m in range(3)], axis=1)
        act4[r] = jnp.concatenate([before, even, odd, after], axis=1).astype(bf)

    activate(0, top[0], 0, False)
    activate(17, bot[0], 1, False)

    @pl.when(scal[2] == 0)
    def _():
        act4[0] = jnp.zeros((64, 1536), bf)

    @pl.when(scal[2] == 15)
    def _():
        act4[17] = jnp.zeros((64, 1536), bf)

    def act_group(g):
        for t in range(4):
            activate(4 * g + t + 1, fine[4 * g + t], (4 * g + t + 2) % 8, True)

    def conv_group(g):
        lhs = jnp.concatenate(
            [
                jnp.concatenate(
                    [act4[4 * g + a : 4 * g + a + 4, :, q * 384 : q * 384 + 1152].reshape(256, 1152) for a in range(3)],
                    axis=1,
                )
                for q in range(2)
            ],
            axis=0,
        )
        out = dot(lhs, cw[...])
        for t in range(4):
            r = 4 * g + t
            for q in range(2):
                o = out[q * 256 + t * 64 : q * 256 + t * 64 + 64] + raw[r, q].astype(f32)
                conv_out[r, q] = o.astype(bf)
                edge[q, r : r + 1] = o[0:1] if q == 0 else o[63:64]

    act_group(0)
    for g in range(4):
        if g < 3:
            act_group(g + 1)
        conv_group(g)


def conv_main(scal, fine, top, bot, cw):
    return call(
        conv_body, "conv_main",
        [jax.ShapeDtypeStruct((16, 2, 64, 384), bf), jax.ShapeDtypeStruct((2, 16, 384), f32)],
        [pltpu.VMEM((18, 64, 1536), bf), pltpu.VMEM((16, 2, 64, 384), bf), pltpu.VMEM((8, 3, 128, 128), f32),
         pltpu.VMEM((8, 2, 3, 80, 128), f32)],
        26, 6_000_000_000, 8_000_000, (scal, fine, top, bot, cw))


def merge_body(scal, conv_in, edge, left, right, cw, mw, conv_out, coarse, sides, nb):
    rows = lax.broadcasted_iota(jnp.int32, (18, 1), 0)
    lat = scal[2]
    on = jnp.logical_and(jnp.logical_or(rows > 0, lat > 0), jnp.logical_or(rows < 17, lat < 15))
    row16 = lax.broadcasted_iota(jnp.int32, (16, 1), 0)
    for q, (ref, tap, at) in enumerate(((left, 0, 0), (right, 2, 48))):
        sides[q] = jnp.where(on, silu_norm(ref[...].astype(f32)), 0.0)
        fixed = edge[q]
        for a in range(3):
            k = a * 1152 + tap * 384
            fixed = fixed + dot(sides[q, a : a + 16].astype(bf), cw[k : k + 384])
        pick = row16 == (0 if q == 0 else 15)
        conv_out[:, 1 - q] = conv_in[:, 1 - q] if q == 0 else conv_out[:, 1 - q]
        if q == 0:
            conv_out[:, 0] = conv_in[:, 0]
        for r in range(16):
            old = conv_out[r, q, at : at + 16].astype(f32)
            conv_out[r, q, at : at + 16] = jnp.where(pick, fixed[r : r + 1], old).astype(bf)

    def normed(i):
        blk = jnp.concatenate([conv_out[2 * i + p, q].astype(f32) for q in range(2) for p in range(2)], axis=1)
        nb[i] = norm(blk).astype(bf)

    def merged(h):
        coarse[4 * h : 4 * h + 4] = dot(nb[4 * h : 4 * h + 4].reshape(256, 1536), mw[...]).astype(bf).reshape(4, 64, 1024)

    for i in range(8):
        normed(i)
        if i == 4:
            merged(0)
    merged(1)


def merge_main(scal, conv, edge, left, right, cw, mw):
    return call(
        merge_body, "merge_main",
        [jax.ShapeDtypeStruct((16, 2, 64, 384), bf), jax.ShapeDtypeStruct((8, 64, 1024), bf)],
        [pltpu.VMEM((2, 18, 384), f32), pltpu.VMEM((8, 64, 1536), bf)],
        26, 1_700_000_000, 12_000_000, (scal, conv, edge, left, right, cw, mw))


def attend_body(scal, own, rows, right, diag, bias_in, scale, qw, pw, mixed, ext, side, xr, xn, qkv, att, bias, ones):
    s, c, lat = scal[0], scal[1], scal[2]
    up = s <= 4
    o_at, r_at, start = jnp.where(up, 0, 4), jnp.where(up, 8, 0), jnp.where(up, s, s - 4)
    ext[pl.ds(o_at, 8)] = own[...]
    ext[pl.ds(r_at, 4)] = rows[...]
    side[pl.ds(o_at, 8)] = right[...].astype(f32)
    side[pl.ds(r_at, 4)] = diag[...].astype(f32)
    hi = lax.broadcasted_iota(jnp.int32, (256, 256), 0) // 64
    hj = lax.broadcasted_iota(jnp.int32, (256, 256), 1) // 64
    ones[...] = jnp.where(hi == hj, 1.0, 0.0).astype(bf)
    kr = lax.broadcasted_iota(jnp.int32, (64, 128), 0) // 8
    qr = (lax.broadcasted_iota(jnp.int32, (64, 128), 1) % 64) // 8
    cut = jnp.where(jnp.where(up, lat == 15, lat == 0), 8 - s, 8)
    ok = (kr >= cut) == (qr >= cut)
    for p in range(8):
        bias[p] = jnp.where(ok, bias_in[p], MASKED)
    for r in range(8):
        row = jnp.concatenate([ext[start + r].astype(f32), side[start + r]], axis=0)
        row = pltpu.roll(row, 72 - c, axis=0)[:64]
        xr[:, r] = row.reshape(8, 8, 1024)
    for w in range(8):
        xn[w * 64 : w * 64 + 64] = norm(xr[w].reshape(64, 1024)).astype(bf)

    def project(n):
        return dot(xn[...], qw[:, n * 512 : n * 512 + 512])

    def scaled(n, t):
        for h in range(2):
            th = t[:, h * 256 : h * 256 + 256]
            ss = dot((th * th).astype(bf), ones[...])
            qkv[:, n * 512 + h * 256 : n * 512 + h * 256 + 256] = (th * lax.rsqrt(ss + QK_EPS)).astype(bf)

    t = project(0)
    for n in range(6):
        nxt = project(n + 1) if n < 5 else None
        if n < 4:
            scaled(n, t)
        else:
            qkv[:, n * 512 : n * 512 + 512] = t.astype(bf)
        t = nxt

    first = lax.broadcasted_iota(jnp.int32, (64, 128), 1) < 64

    def scores(w):
        out = []
        for p in range(8):
            q = qkv[w * 64 : w * 64 + 64, p * 128 : p * 128 + 128]
            k = qkv[w * 64 : w * 64 + 64, 1024 + p * 128 : 1024 + p * 128 + 128]
            z = jnp.zeros_like(q)
            out.append(dot(k, jnp.concatenate([jnp.where(first, q, z), jnp.where(first, z, q)], axis=0), NT))
        return out

    def softmax(st, p):
        st = st * scale[p : p + 1] + bias[p]
        e = jnp.exp(st - jnp.max(st, axis=0, keepdims=True))
        return (e * (1.0 / jnp.sum(e, axis=0, keepdims=True))).astype(bf)

    def out_proj(h):
        a = att[h * 256 : h * 256 + 256]
        m = dot(a, pw[...]) + xr[4 * h : 4 * h + 4].reshape(256, 1024)
        m = m.reshape(4, 8, 8, 1024)
        for r in range(8):
            mixed[r, h * 32 : h * 32 + 32] = m[:, r].reshape(32, 1024).astype(bf)

    nxt = scores(0)
    for w in range(8):
        sts = nxt
        nxt = scores(w + 1) if w < 7 else None
        probs = [softmax(st, p) for p, st in enumerate(sts)]
        outs = [dot(probs[p], qkv[w * 64 : w * 64 + 64, 2048 + p * 128 : 2048 + p * 128 + 128], TN) for p in range(8)]
        for p, o in enumerate(outs):
            att[w * 64 : w * 64 + 64, p * 128 : p * 128 + 128] = jnp.where(first, o[:64], o[64:]).astype(bf)
        if w == 4:
            out_proj(0)
    out_proj(1)


def attend(scal, own, rows, right, diag, bias, scale, qw, pw):
    return call(
        attend_body, "window_attention", jax.ShapeDtypeStruct((8, 64, 1024), bf),
        [pltpu.VMEM((12, 64, 1024), bf), pltpu.VMEM((12, 8, 1024), f32), pltpu.VMEM((8, 8, 8, 1024), f32),
         pltpu.VMEM((512, 1024), bf), pltpu.VMEM((512, 3072), bf), pltpu.VMEM((512, 1024), bf),
         pltpu.VMEM((8, 64, 128), f32), pltpu.VMEM((256, 256), bf)],
        34, 4_500_000_000, 12_000_000, (scal, own, rows, right, diag, bias, scale, qw, pw))


def spread_body(scal, own, rows, left, diag, conv_out, uw, out, ext, side, xs, buf):
    s, c = scal[0], scal[1]
    up = s <= 4
    o_at, r_at, start = jnp.where(up, 4, 0), jnp.where(up, 0, 8), jnp.where(up, 4 - s, 8 - s)
    ext[pl.ds(o_at, 8)] = own[...]
    ext[pl.ds(r_at, 4)] = rows[...]
    side[pl.ds(o_at, 8)] = left[...].astype(f32)
    side[pl.ds(r_at, 4)] = diag[...].astype(f32)
    for i in range(8):
        row = jnp.concatenate([side[start + i], ext[start + i].astype(f32)], axis=0)
        xs[i] = pltpu.roll(row, 64 + c, axis=0)[:64].astype(bf)

    def product(g):
        return dot(xs[2 * g : 2 * g + 2].reshape(128, 1024), uw[...])

    nxt = product(0)
    for g in range(4):
        sp = nxt
        nxt = product(g + 1) if g < 3 else None
        for i in range(2):
            for p in range(2):
                r = 4 * g + 2 * i + p
                slot = r % 4
                for q in range(2):
                    b = 2 * q + p
                    o = conv_out[r, q].astype(f32) + sp[i * 64 : i * 64 + 64, b * 384 : b * 384 + 384]
                    for m, part in enumerate(thirds(o)):
                        buf[slot, m, pl.ds(q, 64, stride=2)] = part
                out[r] = jnp.concatenate([buf[slot, m] for m in range(3)], axis=1).astype(bf)


def spread(scal, own, rows, left, diag, conv_out, uw):
    return call(
        spread_body, "split_tokens", jax.ShapeDtypeStruct((16, 128, 384), bf),
        [pltpu.VMEM((12, 64, 1024), bf), pltpu.VMEM((12, 8, 1024), f32), pltpu.VMEM((8, 64, 1024), bf),
         pltpu.VMEM((4, 3, 128, 128), f32)],
        24, 1_600_000_000, 8_000_000, (scal, own, rows, left, diag, conv_out, uw))


def bias_pairs(pos_bias):
    heads, entries = pos_bias.shape
    position = jnp.arange(WIN * WIN)
    row, col = position // WIN, position % WIN
    relative = (row[None, :] - row[:, None] + WIN - 1) * (2 * WIN - 1) + col[None, :] - col[:, None] + WIN - 1
    one_hot = (relative.reshape(-1)[:, None] == jnp.arange(entries)[None, :]).astype(f32)
    looked = jnp.dot(one_hot, pos_bias.T, precision=lax.Precision.HIGHEST)
    looked = looked.reshape(WIN * WIN, WIN * WIN, heads // 2, 2).transpose(2, 0, 3, 1)
    return looked.reshape(heads // 2, WIN * WIN, 2 * WIN * WIN)


def send(value, lat_step, lon_step):
    lats, lons = lax.axis_size("lat"), lax.axis_size("lon")
    pairs = [
        (a * lons + b, ((a + lat_step) % lats) * lons + (b + lon_step) % lons)
        for a in range(lats)
        for b in range(lons)
    ]
    return lax.ppermute(value, ("lat", "lon"), pairs)


def on_device(fine, conv_weight, merge_weight, qkv_weight, proj_weight, up_weight, logit_scale, pos_bias, shift):
    scal = jnp.concatenate([shift, lax.axis_index("lat").astype(jnp.int32)[None]])
    cw = conv_weight.reshape(3456, 384)
    top = send(fine[15:16], 1, 0)
    bot = send(fine[0:1], -1, 0)
    bias = bias_pairs(pos_bias)
    scale = jnp.repeat(logit_scale.reshape(8, 2), 64, axis=1)
    left = send(jnp.concatenate([top[:, 127], fine[:, 127], bot[:, 127]], axis=0), 0, 1)
    right = send(jnp.concatenate([top[:, 0], fine[:, 0], bot[:, 0]], axis=0), 0, -1)
    conv, edge = conv_main(scal, fine, top, bot, cw)
    conv_out, coarse = merge_main(scal, conv, edge, left, right, cw, merge_weight)
    up = shift[0] <= 4

    def ahead_up(v):
        return send(v[:4], -1, 0), send(v[:, :8], 0, -1), send(v[:4, :8], -1, -1)

    def ahead_down(v):
        return send(v[4:], 1, 0), send(v[:, :8], 0, -1), send(v[4:, :8], 1, -1)

    def behind_up(v):
        return send(v[4:], 1, 0), send(v[:, 56:], 0, 1), send(v[4:, 56:], 1, 1)

    def behind_down(v):
        return send(v[:4], -1, 0), send(v[:, 56:], 0, 1), send(v[:4, 56:], -1, 1)

    rows, side, diag = lax.cond(up, ahead_up, ahead_down, coarse)
    mixed = attend(scal, coarse, rows, side, diag, bias, scale, qkv_weight, proj_weight)
    rows, side, diag = lax.cond(up, behind_up, behind_down, mixed)
    return spread(scal, mixed, rows, side, diag, conv_out, up_weight)


def solution(mesh):
    return jax.shard_map(
        on_device,
        mesh=mesh,
        in_specs=(P("lat", "lon", None), P(), P(), P(), P(), P(), P(), P(), P()),
        out_specs=P("lat", "lon", None),
        check_vma=False,
    )
```

```python
import functools
import jax, jax.numpy as jnp
from jax import lax
from jax.experimental import pallas as pl
from jax.experimental.pallas import tpu as pltpu
from jax.sharding import PartitionSpec as P

bf = jnp.bfloat16
f32 = jnp.float32
WIN = 8
EPS = 1e-5
QK_EPS = 1e-6
MASKED = -1e30
CONV_MIB = 22
BIAS_FLOPS = 12_000_000_000
CONV_FLOPS = 16_000_000_000
HB = pl.BlockSpec(memory_space=pltpu.HBM)
VM = pl.BlockSpec(memory_space=pltpu.VMEM)
SM = pl.BlockSpec(memory_space=pltpu.SMEM)
NT = (((1,), (1,)), ((), ()))
TN = (((0,), (0,)), ((), ()))
NN = (((1,), (0,)), ((), ()))


def dot(a, b, dims=NN):
    return lax.dot_general(a, b, dims, preferred_element_type=f32)


def norm(x):
    c = x - jnp.mean(x, axis=-1, keepdims=True)
    return c * lax.rsqrt(jnp.mean(c * c, axis=-1, keepdims=True) + EPS)


def silu_norm(x):
    n = norm(x)
    return n / (1.0 + jnp.exp(-n))


def thirds(x):
    return [x[..., m * 128 : m * 128 + 128] for m in range(3)]


def call(body, name, outs, scratch, mib, flops, nbytes, scalars, hbm, vmem):
    return pl.pallas_call(
        body,
        out_shape=[jax.ShapeDtypeStruct(shape, dtype) for shape, dtype in outs],
        in_specs=[SM] * len(scalars) + [HB] * len(hbm) + [VM] * len(vmem),
        out_specs=[VM] * len(outs),
        scratch_shapes=scratch,
        compiler_params=pltpu.CompilerParams(vmem_limit_bytes=mib << 20),
        cost_estimate=pl.CostEstimate(flops=flops, bytes_accessed=nbytes, transcendentals=0),
        name=name,
    )(*scalars, *hbm, *vmem)


def halves(shift):
    s = shift[0]
    up = s <= 4
    base = jnp.where(up, 0, 4)
    return s, up, base, lambda k: jnp.where(up, k < s, k >= s - 4)


def bias_body(shift, lat, pos, out, table):
    s, up, base, _ = halves(shift)
    sigma = s - base
    entry = lax.broadcasted_iota(jnp.int32, (225, 1024), 0)
    col = lax.broadcasted_iota(jnp.int32, (225, 1024), 1)
    lane_in = col % 128
    want = (lane_in // 8) * 15 + lane_in % 8 - col // 128 + 7
    one_hot = jnp.where(jnp.logical_and(entry == want, lane_in < 120), 1.0, 0.0).astype(f32)
    looked = lax.dot_general(pos[...], one_hot, NN, precision=lax.Precision.HIGHEST, preferred_element_type=f32)
    for cb in range(8):
        table[cb] = looked[:, cb * 128 : cb * 128 + 128]
    lane = lax.broadcasted_iota(jnp.int32, (8, 128), 1)
    low = lane < 64
    last = jnp.where(up, lat[0] == 15, lat[0] == 0)
    cut = jnp.where(last, 8 - s, 8)
    q_row = ((lane % 64) // 8 - sigma + 8) % 8
    q_late = q_row >= cut
    for p in range(8):
        pair = [table[:, 2 * p + i] for i in range(2)]
        for rb in range(8):
            turned = []
            for t in pair:
                t = pltpu.roll(t, (128 - (7 - rb) * 8) % 128, axis=1) if rb < 7 else t
                t = jnp.where(low, t, pltpu.roll(t, 64, axis=1))
                turned.append(pltpu.roll(t, 8 * sigma, axis=1))
            row = jnp.where(low, turned[0], turned[1])
            row = jnp.where(q_late == (rb >= cut), row, MASKED)
            out[p, (rb + sigma) % 8] = row


def bias_table(shift, lat, pos):
    return call(bias_body, "bias_table", [((8, 8, 8, 128), f32)], [pltpu.VMEM((8, 16, 128), f32)], 8, BIAS_FLOPS, 300_000,
                (shift, lat), (), (pos,))[0].reshape(8, 64, 128)


def conv_body(lat, fine, cw, top, bot, conv_out, edge, act4, raw, split, shift):
    zero_row = jnp.zeros((1, 128), f32)
    for slot in range(8):
        for m in range(3):
            shift[slot, 0, m, 7:8] = zero_row
            shift[slot, 1, m, 72:73] = zero_row

    def activate(r, x, slot, keep):
        for m, part in enumerate(thirds(x.astype(f32))):
            split[slot, m] = part
        even, odd = [
            jnp.concatenate([split[slot, m, pl.ds(q, 64, stride=2)] for m in range(3)], axis=1) for q in range(2)
        ]
        if keep:
            raw[r - 1, 0] = even.astype(bf)
            raw[r - 1, 1] = odd.astype(bf)
        even, odd = silu_norm(even), silu_norm(odd)
        for m in range(3):
            shift[slot, 0, m, 8:72] = odd[:, m * 128 : m * 128 + 128]
            shift[slot, 1, m, 8:72] = even[:, m * 128 : m * 128 + 128]
        before = jnp.concatenate([shift[slot, 0, m, 7:71] for m in range(3)], axis=1)
        after = jnp.concatenate([shift[slot, 1, m, 9:73] for m in range(3)], axis=1)
        act4[r] = jnp.concatenate([before, even, odd, after], axis=1).astype(bf)

    activate(0, top[0], 0, False)
    activate(17, bot[0], 1, False)

    @pl.when(lat[0] == 0)
    def _():
        act4[0] = jnp.zeros((64, 1536), bf)

    @pl.when(lat[0] == 15)
    def _():
        act4[17] = jnp.zeros((64, 1536), bf)

    def act_group(g):
        for t in range(4):
            activate(4 * g + t + 1, fine[4 * g + t], (4 * g + t + 2) % 8, True)

    def conv_group(g):
        lhs = jnp.concatenate(
            [
                jnp.concatenate(
                    [act4[4 * g + a : 4 * g + a + 4, :, q * 384 : q * 384 + 1152].reshape(256, 1152) for a in range(3)],
                    axis=1,
                )
                for q in range(2)
            ],
            axis=0,
        )
        out = dot(lhs, cw[...])
        for t in range(4):
            r = 4 * g + t
            for q in range(2):
                o = out[q * 256 + t * 64 : q * 256 + t * 64 + 64] + raw[r, q].astype(f32)
                conv_out[r, q] = o.astype(bf)
                edge[q, r : r + 1] = o[0:1] if q == 0 else o[63:64]

    act_group(0)
    act_group(1)
    conv_group(0)
    act_group(2)
    conv_group(1)
    act_group(3)
    conv_group(2)
    conv_group(3)


def conv_main(lat, fine, cw, top, bot):
    return call(
        conv_body, "conv_main", [((16, 2, 64, 384), bf), ((2, 16, 384), f32)],
        [pltpu.VMEM((18, 64, 1536), bf), pltpu.VMEM((16, 2, 64, 384), bf), pltpu.VMEM((8, 3, 128, 128), f32),
         pltpu.VMEM((8, 2, 3, 80, 128), f32)],
        CONV_MIB, CONV_FLOPS, 8_000_000, (lat,), (), (fine, cw, top, bot))


def block_norm(conv, i, cols):
    blk = [conv[2 * i + p, q, 0 : max(cols, 16)].astype(f32)[:cols] for q in range(2) for p in range(2)]
    return norm(jnp.concatenate(blk, axis=1))


def merge_body(shift, lat, conv_in, edge, left, right, cw, mw, conv_out, coarse, side, corner, sides, nb):
    _, _, base, _ = halves(shift)
    rows = lax.broadcasted_iota(jnp.int32, (18, 1), 0)
    on = jnp.logical_and(jnp.logical_or(rows > 0, lat[0] > 0), jnp.logical_or(rows < 17, lat[0] < 15))
    row16 = lax.broadcasted_iota(jnp.int32, (16, 1), 0)
    conv_out[...] = conv_in[...]
    for q, ref in enumerate((left, right)):
        sides[q] = jnp.where(on, silu_norm(ref[...].astype(f32)), 0.0)
    for q, at in enumerate((0, 48)):
        fixed = edge[q]
        for a in range(3):
            k = a * 1152 + q * 768
            fixed = fixed + dot(sides[q, a : a + 16].astype(bf), cw[k : k + 384])
        pick = row16 == (0 if q == 0 else 15)
        for r in range(16):
            old = conv_in[r, q, at : at + 16].astype(f32)
            conv_out[r, q, at : at + 16] = jnp.where(pick, fixed[r : r + 1], old).astype(bf)
    for k in range(4):
        nb[k * 64 : k * 64 + 64] = block_norm(conv_out, base + k, 64).astype(bf)
    nb[256:288] = jnp.concatenate([block_norm(conv_out, 4 - base + k, 8) for k in range(4)], axis=0).astype(bf)
    out = dot(nb[...], mw[...])
    coarse[...] = out[:256].astype(bf).reshape(4, 64, 1024)
    for k in range(4):
        corner[k] = out[k * 64 : k * 64 + 8].astype(bf)
        side[k] = out[k * 64 : k * 64 + 8].astype(bf)
        side[4 + k] = out[256 + k * 8 : 264 + k * 8].astype(bf)


def merge_moved(shift, lat, conv, edge, left, right, cw, mw):
    return call(
        merge_body, "merge_moved",
        [((16, 2, 64, 384), bf), ((4, 64, 1024), bf), ((8, 8, 1024), bf), ((4, 8, 1024), bf)],
        [pltpu.VMEM((2, 18, 384), f32), pltpu.VMEM((288, 1536), bf)],
        22, 1_000_000_000, 9_000_000, (shift, lat), (), (conv, edge, left, right, cw, mw))


def head_ones():
    hi = lax.broadcasted_iota(jnp.int32, (256, 256), 0) // 64
    hj = lax.broadcasted_iota(jnp.int32, (256, 256), 1) // 64
    return jnp.where(hi == hj, 1.0, 0.0).astype(bf)


def project_heads(xn, qw, ones, qkv):
    def project(n):
        return dot(xn[...], qw[:, n * 512 : n * 512 + 512])

    t = project(0)
    for n in range(6):
        nxt = project(n + 1) if n < 5 else None
        if n < 4:
            for h in range(2):
                at = n * 512 + h * 256
                th = t[:, h * 256 : h * 256 + 256]
                ss = dot((th * th).astype(bf), ones[...])
                qkv[:, at : at + 256] = (th * lax.rsqrt(ss + QK_EPS)).astype(bf)
        else:
            qkv[:, n * 512 : n * 512 + 512] = t.astype(bf)
        t = nxt


def kept_body(shift, conv, mw, qw, tail, xr, qkv, nb, xn, ones, merged):
    _, _, base, _ = halves(shift)
    c = shift[1]
    ones[...] = head_ones()
    for k in range(4):
        nb[k * 64 : k * 64 + 64] = block_norm(conv, 4 - base + k, 64).astype(bf)
    @pl.loop(0, 2)
    def _(n):
        cols = pl.ds(pl.multiple_of(n * 512, 512), 512)
        merged[:, cols] = dot(nb[...], mw[:, cols])

    coarse = merged[...].astype(bf).astype(f32)
    rows = []
    for k in range(4):
        row = coarse[k * 64 : k * 64 + 64]
        tail[k] = row[56:].astype(bf)
        rows.append(pltpu.roll(row, 64 - c, axis=0))
    for w in range(7):
        x = jnp.concatenate([row[w * 8 : w * 8 + 8] for row in rows], axis=0)
        xr[w] = x.astype(bf)
        xn[w * 32 : w * 32 + 32] = norm(x).astype(bf)

    @pl.loop(0, 4)
    def _(n):
        for h in range(2):
            cols = pl.ds(pl.multiple_of(n * 512 + h * 256, 256), 256)
            t = dot(xn[...], qw[:, cols])
            ss = dot((t * t).astype(bf), ones[...])
            qkv[:, cols] = (t * lax.rsqrt(ss + QK_EPS)).astype(bf)

    @pl.loop(4, 6)
    def _(n):
        cols = pl.ds(pl.multiple_of(n * 512, 512), 512)
        qkv[:, cols] = dot(xn[...], qw[:, cols]).astype(bf)


def kept(shift, conv, mw, qw):
    return call(
        kept_body, "kept_rows", [((4, 8, 1024), bf), ((7, 32, 1024), bf), ((224, 3072), bf)],
        [pltpu.VMEM((256, 1536), bf), pltpu.VMEM((224, 1024), bf), pltpu.VMEM((256, 256), bf), pltpu.VMEM((256, 1024), f32)],
        28, 2_500_000_000, 14_000_000, (shift,), (), (conv, mw, qw))


def attend_body(shift, scale, own, rows, side, diag, tail, xr_b, qkv_b, bias, qw, pw,
                mixed, mixed_side, corner, att_b, xr, xn, qkv, att, ones):
    s, up, base, received = halves(shift)
    c = shift[1]
    ones[...] = head_ones()
    turned = []
    for k in range(4):
        got = received(k)
        row = jnp.concatenate(
            [jnp.where(got, rows[k], own[k]).astype(f32),
             jnp.where(got, diag[k], side[k]).astype(f32)], axis=0)
        turned.append(pltpu.roll(row, 72 - c, axis=0))
    for w in range(8):
        x = jnp.concatenate([row[w * 8 : w * 8 + 8] for row in turned], axis=0)
        xr[w * 32 : w * 32 + 32] = x
        xn[w * 32 : w * 32 + 32] = norm(x).astype(bf)
    ends = [
        pltpu.roll(jnp.concatenate([tail[k].astype(f32), side[4 + k].astype(f32)], axis=0), 16 - c, axis=0)[:8]
        for k in range(4)
    ]
    x = jnp.concatenate(ends, axis=0)
    xr[256:288] = x
    xn[256:288] = norm(x).astype(bf)
    project_heads(xn, qw, ones, qkv)

    lane = lax.broadcasted_iota(jnp.int32, (64, 128), 1)
    first = lane < 64
    low = lax.broadcasted_iota(jnp.int32, (1, 128), 1) < 64

    def part(w, at):
        other = qkv_b[w * 32 : w * 32 + 32, at : at + 128] if w < 7 else qkv[256:288, at : at + 128]
        return jnp.concatenate([qkv[w * 32 : w * 32 + 32, at : at + 128], other], axis=0)

    def scores(w):
        out = []
        for p in range(8):
            q = part(w, p * 128)
            z = jnp.zeros_like(q)
            q = jnp.concatenate([jnp.where(first, q, z), jnp.where(first, z, q)], axis=0)
            out.append(dot(part(w, 1024 + p * 128), q, NT))
        return out

    def softmax(st, p):
        st = st * jnp.where(low, scale[2 * p], scale[2 * p + 1]) + bias[p]
        e = jnp.exp(st - jnp.max(st, axis=0, keepdims=True))
        return (e * (1.0 / jnp.sum(e, axis=0, keepdims=True))).astype(bf)

    nxt = scores(0)
    for w in range(8):
        sts = nxt
        nxt = scores(w + 1) if w < 7 else None
        probs = [softmax(st, p) for p, st in enumerate(sts)]
        outs = [dot(probs[p], part(w, 2048 + p * 128), TN) for p in range(8)]
        for p, o in enumerate(outs):
            o = jnp.where(first, o[:64], o[64:]).astype(bf)
            at = slice(p * 128, p * 128 + 128)
            att[w * 32 : w * 32 + 32, at] = o[:32]
            if w < 7:
                att_b[w * 32 : w * 32 + 32, at] = o[32:]
            else:
                att[256:288, at] = o[32:]
    m = dot(att[...], pw[...]) + xr[...]
    for k in range(4):
        mixed[k] = jnp.concatenate([m[w * 32 + k * 8 : w * 32 + k * 8 + 8] for w in range(8)], axis=0).astype(bf)
        corner[k] = m[224 + k * 8 : 232 + k * 8].astype(bf)
        mixed_side[k] = m[224 + k * 8 : 232 + k * 8].astype(bf)
        mixed_side[4 + k] = m[256 + k * 8 : 264 + k * 8].astype(bf)


def attend(shift, scale, own, rows, side, diag, tail, xr_b, qkv_b, bias, qw, pw):
    return call(
        attend_body, "window_attention", [((4, 64, 1024), bf), ((8, 8, 1024), bf), ((4, 8, 1024), bf), ((224, 1024), bf)],
        [pltpu.VMEM((288, 1024), f32), pltpu.VMEM((288, 1024), bf), pltpu.VMEM((288, 3072), bf),
         pltpu.VMEM((288, 1024), bf), pltpu.VMEM((256, 256), bf)],
        30, 3_500_000_000, 14_000_000, (shift, scale), (),
        (own, rows, side, diag, tail, xr_b, qkv_b, bias, qw, pw))


def interleaved(buf, slot, conv_rows, sp, b0, n):
    for q in range(2):
        o = conv_rows[q] + sp[:, (2 * q + b0) * 384 : (2 * q + b0) * 384 + 384]
        for m, part in enumerate(thirds(o)):
            buf[slot, m, pl.ds(q, n, stride=2)] = part
    return jnp.concatenate([buf[slot, m, 0 : 2 * n] for m in range(3)], axis=1).astype(bf)


def kept_out_body(shift, att, xr, side, conv, pw, uw, out, head, xs, buf):
    _, _, base, _ = halves(shift)
    c = shift[1]
    m = dot(att[...], pw[...]) + xr[...].reshape(224, 1024).astype(f32)
    for k in range(4):
        row = jnp.concatenate([m[w * 32 + k * 8 : w * 32 + k * 8 + 8] for w in range(7)] + [side[4 + k].astype(f32)], axis=0)
        head[k] = row[:8].astype(bf)
        xs[k] = pltpu.roll(row, c, axis=0).astype(bf)
    for g in range(2):
        sp = dot(xs[2 * g : 2 * g + 2].reshape(128, 1024), uw[...])
        for i in range(2):
            k = 2 * g + i
            for p in range(2):
                r = 2 * (4 - base + k) + p
                cr = [conv[r, q].astype(f32) for q in range(2)]
                out[2 * k + p] = interleaved(buf, (2 * k + p) % 4, cr, sp[i * 64 : i * 64 + 64], p, 64)


def kept_out(shift, att, xr, side, conv, pw, uw):
    return call(
        kept_out_body, "kept_out", [((8, 128, 384), bf), ((4, 8, 1024), bf)],
        [pltpu.VMEM((4, 64, 1024), bf), pltpu.VMEM((4, 3, 128, 128), f32)],
        20, 1_300_000_000, 8_000_000, (shift,), (), (att, xr, side, conv, pw, uw))


def moved_out_body(shift, own, rows, left, diag, head, res, conv, uw, out, xs, buf):
    _, up, base, received = halves(shift)
    c = shift[1]
    for k in range(4):
        got = received(k)
        row = jnp.concatenate(
            [jnp.where(got, diag[k], left[k]).astype(f32),
             jnp.where(got, rows[k], own[k]).astype(f32)], axis=0)
        xs[k * 64 : k * 64 + 64] = pltpu.roll(row, 64 + c, axis=0)[:64].astype(bf)
    ends = [
        pltpu.roll(jnp.concatenate([left[4 + k].astype(f32), head[k].astype(f32)], axis=0), 8 + c, axis=0)[:8]
        for k in range(4)
    ]
    xs[256:288] = jnp.concatenate(ends, axis=0).astype(bf)
    sp = dot(xs[...], uw[...])
    for k in range(4):
        for p in range(2):
            r = 2 * (base + k) + p
            cr = [conv[r, q].astype(f32) for q in range(2)]
            out[r] = interleaved(buf, (2 * k + p) % 4, cr, sp[k * 64 : k * 64 + 64], p, 64)
    for k in range(4):
        for p in range(2):
            r = 2 * (4 - base + k) + p
            cr = [conv[r, q, 0:16].astype(f32)[:8] for q in range(2)]
            out[r] = res[2 * k + p]
            out[r, 0:16] = interleaved(buf, (2 * k + p) % 4, cr, sp[256 + k * 8 : 264 + k * 8], p, 8)


def moved_out(shift, own, rows, left, diag, head, res, conv, uw):
    return call(
        moved_out_body, "moved_out", [((16, 128, 384), bf)],
        [pltpu.VMEM((288, 1024), bf), pltpu.VMEM((4, 3, 128, 128), f32)],
        24, 1_000_000_000, 9_000_000, (shift,), (), (own, rows, left, diag, head, res, conv, uw))[0]


def send(value, lat_step, lon_step):
    lats, lons = lax.axis_size("lat"), lax.axis_size("lon")
    pairs = [
        (a * lons + b, ((a + lat_step) % lats) * lons + (b + lon_step) % lons)
        for a in range(lats)
        for b in range(lons)
    ]
    return lax.ppermute(value, ("lat", "lon"), pairs)


def on_device(fine, conv_weight, merge_weight, qkv_weight, proj_weight, up_weight, logit_scale, pos_bias, shift):
    lat = lax.axis_index("lat").astype(jnp.int32).reshape(1)
    top = send(fine[15:16], 1, 0)
    bot = send(fine[0:1], -1, 0)
    bias = bias_table(shift, lat, pos_bias)
    left = send(jnp.concatenate([top[:, 127], fine[:, 127], bot[:, 127]], axis=0), 0, 1)
    right = send(jnp.concatenate([top[:, 0], fine[:, 0], bot[:, 0]], axis=0), 0, -1)
    cw, mw, qw, pw, uw = conv_weight.reshape(3456, 384), merge_weight, qkv_weight, proj_weight, up_weight
    conv, edge = conv_main(lat, fine, cw, top, bot)
    conv, moved, side, corner = merge_moved(shift, lat, conv, edge, left, right, cw, mw)
    up = shift[0] <= 4

    def ahead(step):
        def branch(moved, side, corner, conv, mw, qw):
            got = send(moved, step, 0), send(side, 0, -1), send(corner, step, -1)
            return got + tuple(kept(shift, conv, mw, qw))

        return branch

    def behind(step):
        def branch(mixed, side, corner, att_b, xr_b, conv, pw, uw):
            got = send(mixed, step, 0), send(side, 0, 1), send(corner, step, 1)
            return got + tuple(kept_out(shift, att_b, xr_b, side, conv, pw, uw))

        return branch

    rows, side, diag, tail, xr_b, qkv_b = lax.cond(up, ahead(-1), ahead(1), moved, side, corner, conv, mw, qw)
    mixed, mixed_side, corner, att_b = attend(
        shift, logit_scale, moved, rows, side, diag, tail, xr_b, qkv_b, bias, qw, pw)
    rows, side, diag, res, head = lax.cond(up, behind(1), behind(-1), mixed, mixed_side, corner, att_b, xr_b, conv, pw, uw)
    return moved_out(shift, mixed, rows, side, diag, head, res, conv, uw)


def solution(mesh):
    return jax.shard_map(
        on_device,
        mesh=mesh,
        in_specs=(P("lat", "lon", None), P(), P(), P(), P(), P(), P(), P(), P()),
        out_specs=P("lat", "lon", None),
        check_vma=False,
    )
```

```python
import functools
import jax, jax.numpy as jnp
from jax import lax
from jax.experimental import pallas as pl
from jax.experimental.pallas import tpu as pltpu
from jax.sharding import PartitionSpec as P

bf = jnp.bfloat16
f32 = jnp.float32
WIN = 8
EPS = 1e-5
QK_EPS = 1e-6
MASKED = -1e30
CONV_MIB = 22
BIAS_FLOPS = 12_000_000_000
CONV_FLOPS = 16_000_000_000
HB = pl.BlockSpec(memory_space=pltpu.HBM)
VM = pl.BlockSpec(memory_space=pltpu.VMEM)
SM = pl.BlockSpec(memory_space=pltpu.SMEM)
NT = (((1,), (1,)), ((), ()))
TN = (((0,), (0,)), ((), ()))
NN = (((1,), (0,)), ((), ()))


def dot(a, b, dims=NN):
    return lax.dot_general(a, b, dims, preferred_element_type=f32)


def norm(x):
    c = x - jnp.mean(x, axis=-1, keepdims=True)
    return c * lax.rsqrt(jnp.mean(c * c, axis=-1, keepdims=True) + EPS)


def silu_norm(x):
    n = norm(x)
    return n / (1.0 + jnp.exp(-n))


def thirds(x):
    return [x[..., m * 128 : m * 128 + 128] for m in range(3)]


def call(body, name, outs, scratch, mib, flops, nbytes, scalars, hbm, vmem):
    return pl.pallas_call(
        body,
        out_shape=[jax.ShapeDtypeStruct(shape, dtype) for shape, dtype in outs],
        in_specs=[SM] * len(scalars) + [HB] * len(hbm) + [VM] * len(vmem),
        out_specs=[VM] * len(outs),
        scratch_shapes=scratch,
        compiler_params=pltpu.CompilerParams(vmem_limit_bytes=mib << 20),
        cost_estimate=pl.CostEstimate(flops=flops, bytes_accessed=nbytes, transcendentals=0),
        name=name,
    )(*scalars, *hbm, *vmem)


def halves(shift):
    s = shift[0]
    up = s <= 4
    base = jnp.where(up, 0, 4)
    return s, up, base, lambda k: jnp.where(up, k < s, k >= s - 4)


def bias_body(shift, lat, pos, out, table):
    s, up, base, _ = halves(shift)
    sigma = s - base
    entry = lax.broadcasted_iota(jnp.int32, (225, 1024), 0)
    col = lax.broadcasted_iota(jnp.int32, (225, 1024), 1)
    lane_in = col % 128
    want = (lane_in // 8) * 15 + lane_in % 8 - col // 128 + 7
    one_hot = jnp.where(jnp.logical_and(entry == want, lane_in < 120), 1.0, 0.0).astype(f32)
    looked = lax.dot_general(pos[...], one_hot, NN, precision=lax.Precision.HIGHEST, preferred_element_type=f32)
    for cb in range(8):
        table[cb] = looked[:, cb * 128 : cb * 128 + 128]
    lane = lax.broadcasted_iota(jnp.int32, (8, 128), 1)
    low = lane < 64
    last = jnp.where(up, lat[0] == 15, lat[0] == 0)
    cut = jnp.where(last, 8 - s, 8)
    q_row = ((lane % 64) // 8 - sigma + 8) % 8
    q_late = q_row >= cut
    for p in range(8):
        pair = [table[:, 2 * p + i] for i in range(2)]
        for rb in range(8):
            turned = []
            for t in pair:
                t = pltpu.roll(t, (128 - (7 - rb) * 8) % 128, axis=1) if rb < 7 else t
                t = jnp.where(low, t, pltpu.roll(t, 64, axis=1))
                turned.append(pltpu.roll(t, 8 * sigma, axis=1))
            row = jnp.where(low, turned[0], turned[1])
            row = jnp.where(q_late == (rb >= cut), row, MASKED)
            out[p, (rb + sigma) % 8] = row


def bias_table(shift, lat, pos):
    return call(bias_body, "bias_table", [((8, 8, 8, 128), f32)], [pltpu.VMEM((8, 16, 128), f32)], 8, BIAS_FLOPS, 300_000,
                (shift, lat), (), (pos,))[0].reshape(8, 64, 128)


def conv_body(lat, fine, cw, top, bot, conv_out, edge, act4, raw, split, shift):
    zero_row = jnp.zeros((1, 128), f32)
    for slot in range(8):
        for m in range(3):
            shift[slot, 0, m, 7:8] = zero_row
            shift[slot, 1, m, 72:73] = zero_row

    def activate(r, x, slot, keep):
        for m, part in enumerate(thirds(x.astype(f32))):
            split[slot, m, 0:128] = part
        even, odd = [
            jnp.concatenate([split[slot, m, pl.ds(q, 64, stride=2)] for m in range(3)], axis=1) for q in range(2)
        ]
        if keep:
            raw[r - 1, 0] = even.astype(bf)
            raw[r - 1, 1] = odd.astype(bf)
        even, odd = silu_norm(even), silu_norm(odd)
        for m in range(3):
            shift[slot, 0, m, 8:72] = odd[:, m * 128 : m * 128 + 128]
            shift[slot, 1, m, 8:72] = even[:, m * 128 : m * 128 + 128]
        before = jnp.concatenate([shift[slot, 0, m, 7:71] for m in range(3)], axis=1)
        after = jnp.concatenate([shift[slot, 1, m, 9:73] for m in range(3)], axis=1)
        act4[r] = jnp.concatenate([before, even, odd, after], axis=1).astype(bf)

    activate(0, top[0], 0, False)
    activate(17, bot[0], 1, False)

    @pl.when(lat[0] == 0)
    def _():
        act4[0] = jnp.zeros((64, 1536), bf)

    @pl.when(lat[0] == 15)
    def _():
        act4[17] = jnp.zeros((64, 1536), bf)

    def act_group(g):
        for t in range(4):
            activate(4 * g + t + 1, fine[4 * g + t], (4 * g + t + 2) % 8, True)

    def conv_group(g):
        lhs = jnp.concatenate(
            [
                jnp.concatenate(
                    [act4[4 * g + a : 4 * g + a + 4, :, q * 384 : q * 384 + 1152].reshape(256, 1152) for a in range(3)],
                    axis=1,
                )
                for q in range(2)
            ],
            axis=0,
        )
        out = dot(lhs, cw[...])
        for t in range(4):
            r = 4 * g + t
            for q in range(2):
                o = out[q * 256 + t * 64 : q * 256 + t * 64 + 64] + raw[r, q].astype(f32)
                conv_out[r, q] = o.astype(bf)
                edge[q, r : r + 1] = o[0:1] if q == 0 else o[63:64]

    act_group(0)
    act_group(1)
    conv_group(0)
    act_group(2)
    conv_group(1)
    act_group(3)
    conv_group(2)
    conv_group(3)


def conv_main(lat, fine, cw, top, bot):
    return call(
        conv_body, "conv_main", [((16, 2, 64, 384), bf), ((2, 16, 384), f32)],
        [pltpu.VMEM((18, 64, 1536), bf), pltpu.VMEM((16, 2, 64, 384), bf), pltpu.VMEM((8, 3, 136, 128), f32),
         pltpu.VMEM((8, 2, 3, 80, 128), f32)],
        CONV_MIB, CONV_FLOPS, 8_000_000, (lat,), (), (fine, cw, top, bot))


def block_norm(conv, i, cols):
    blk = [conv[2 * i + p, q, 0 : max(cols, 16)].astype(f32)[:cols] for q in range(2) for p in range(2)]
    return norm(jnp.concatenate(blk, axis=1))


def merge_body(shift, lat, conv_in, edge, left, right, cw, mw, conv_out, coarse, side, corner, sides, nb):
    _, _, base, _ = halves(shift)
    rows = lax.broadcasted_iota(jnp.int32, (18, 1), 0)
    on = jnp.logical_and(jnp.logical_or(rows > 0, lat[0] > 0), jnp.logical_or(rows < 17, lat[0] < 15))
    row16 = lax.broadcasted_iota(jnp.int32, (16, 1), 0)
    conv_out[...] = conv_in[...]
    for q, ref in enumerate((left, right)):
        sides[q] = jnp.where(on, silu_norm(ref[...].astype(f32)), 0.0)
    for q, at in enumerate((0, 48)):
        fixed = edge[q]
        for a in range(3):
            k = a * 1152 + q * 768
            fixed = fixed + dot(sides[q, a : a + 16].astype(bf), cw[k : k + 384])
        pick = row16 == (0 if q == 0 else 15)
        for r in range(16):
            old = conv_in[r, q, at : at + 16].astype(f32)
            conv_out[r, q, at : at + 16] = jnp.where(pick, fixed[r : r + 1], old).astype(bf)
    for k in range(4):
        nb[k * 64 : k * 64 + 64] = block_norm(conv_out, base + k, 64).astype(bf)
    nb[256:288] = jnp.concatenate([block_norm(conv_out, 4 - base + k, 8) for k in range(4)], axis=0).astype(bf)
    out = dot(nb[...], mw[...])
    coarse[...] = out[:256].astype(bf).reshape(4, 64, 1024)
    for k in range(4):
        corner[k] = out[k * 64 : k * 64 + 8].astype(bf)
        side[k] = out[k * 64 : k * 64 + 8].astype(bf)
        side[4 + k] = out[256 + k * 8 : 264 + k * 8].astype(bf)


def merge_moved(shift, lat, conv, edge, left, right, cw, mw):
    return call(
        merge_body, "merge_moved",
        [((16, 2, 64, 384), bf), ((4, 64, 1024), bf), ((8, 8, 1024), bf), ((4, 8, 1024), bf)],
        [pltpu.VMEM((2, 18, 384), f32), pltpu.VMEM((288, 1536), bf)],
        22, 1_000_000_000, 9_000_000, (shift, lat), (), (conv, edge, left, right, cw, mw))


def head_ones():
    hi = lax.broadcasted_iota(jnp.int32, (256, 256), 0) // 64
    hj = lax.broadcasted_iota(jnp.int32, (256, 256), 1) // 64
    return jnp.where(hi == hj, 1.0, 0.0).astype(bf)


def project_heads(xn, qw, ones, qkv):
    def project(n):
        return dot(xn[...], qw[:, n * 512 : n * 512 + 512])

    t = project(0)
    for n in range(6):
        nxt = project(n + 1) if n < 5 else None
        if n < 4:
            for h in range(2):
                at = n * 512 + h * 256
                th = t[:, h * 256 : h * 256 + 256]
                ss = dot((th * th).astype(bf), ones[...])
                qkv[:, at : at + 256] = (th * lax.rsqrt(ss + QK_EPS)).astype(bf)
        else:
            qkv[:, n * 512 : n * 512 + 512] = t.astype(bf)
        t = nxt


def kept_body(shift, conv, mw, qw, tail, xr, qkv, nb, xn, ones, merged):
    _, _, base, _ = halves(shift)
    c = shift[1]
    ones[...] = head_ones()
    for k in range(4):
        nb[k * 64 : k * 64 + 64] = block_norm(conv, 4 - base + k, 64).astype(bf)
    @pl.loop(0, 2)
    def _(n):
        cols = pl.ds(pl.multiple_of(n * 512, 512), 512)
        merged[:, cols] = dot(nb[...], mw[:, cols])

    coarse = merged[...].astype(bf).astype(f32)
    rows = []
    for k in range(4):
        row = coarse[k * 64 : k * 64 + 64]
        tail[k] = row[56:].astype(bf)
        rows.append(pltpu.roll(row, 64 - c, axis=0))
    for w in range(7):
        x = jnp.concatenate([row[w * 8 : w * 8 + 8] for row in rows], axis=0)
        xr[w] = x.astype(bf)
        xn[w * 32 : w * 32 + 32] = norm(x).astype(bf)

    @pl.loop(0, 4)
    def _(n):
        for h in range(2):
            cols = pl.ds(pl.multiple_of(n * 512 + h * 256, 256), 256)
            t = dot(xn[...], qw[:, cols])
            ss = dot((t * t).astype(bf), ones[...])
            qkv[:, cols] = (t * lax.rsqrt(ss + QK_EPS)).astype(bf)

    @pl.loop(4, 6)
    def _(n):
        cols = pl.ds(pl.multiple_of(n * 512, 512), 512)
        qkv[:, cols] = dot(xn[...], qw[:, cols]).astype(bf)


def kept(shift, conv, mw, qw):
    return call(
        kept_body, "kept_rows", [((4, 8, 1024), bf), ((7, 32, 1024), bf), ((224, 3072), bf)],
        [pltpu.VMEM((256, 1536), bf), pltpu.VMEM((224, 1024), bf), pltpu.VMEM((256, 256), bf), pltpu.VMEM((256, 1024), f32)],
        28, 2_500_000_000, 14_000_000, (shift,), (), (conv, mw, qw))


def attend_body(shift, scale, own, rows, side, diag, tail, xr_b, qkv_b, bias, qw, pw,
                mixed, mixed_side, corner, att_b, xr, xn, qkv, att, ones):
    s, up, base, received = halves(shift)
    c = shift[1]
    ones[...] = head_ones()
    turned = []
    for k in range(4):
        got = received(k)
        row = jnp.concatenate(
            [jnp.where(got, rows[k], own[k]).astype(f32),
             jnp.where(got, diag[k], side[k]).astype(f32)], axis=0)
        turned.append(pltpu.roll(row, 72 - c, axis=0))
    for w in range(8):
        x = jnp.concatenate([row[w * 8 : w * 8 + 8] for row in turned], axis=0)
        xr[w * 32 : w * 32 + 32] = x
        xn[w * 32 : w * 32 + 32] = norm(x).astype(bf)
    ends = [
        pltpu.roll(jnp.concatenate([tail[k].astype(f32), side[4 + k].astype(f32)], axis=0), 16 - c, axis=0)[:8]
        for k in range(4)
    ]
    x = jnp.concatenate(ends, axis=0)
    xr[256:288] = x
    xn[256:288] = norm(x).astype(bf)
    project_heads(xn, qw, ones, qkv)

    lane = lax.broadcasted_iota(jnp.int32, (64, 128), 1)
    first = lane < 64
    low = lax.broadcasted_iota(jnp.int32, (1, 128), 1) < 64

    def part(w, at):
        other = qkv_b[w * 32 : w * 32 + 32, at : at + 128] if w < 7 else qkv[256:288, at : at + 128]
        return jnp.concatenate([qkv[w * 32 : w * 32 + 32, at : at + 128], other], axis=0)

    def scores(w):
        out = []
        for p in range(8):
            q = part(w, p * 128)
            z = jnp.zeros_like(q)
            q = jnp.concatenate([jnp.where(first, q, z), jnp.where(first, z, q)], axis=0)
            out.append(dot(part(w, 1024 + p * 128), q, NT))
        return out

    def softmax(st, p):
        st = st * jnp.where(low, scale[2 * p], scale[2 * p + 1]) + bias[p]
        e = jnp.exp(st - jnp.max(st, axis=0, keepdims=True))
        return (e * (1.0 / jnp.sum(e, axis=0, keepdims=True))).astype(bf)

    nxt = scores(0)
    for w in range(8):
        sts = nxt
        nxt = scores(w + 1) if w < 7 else None
        probs = [softmax(st, p) for p, st in enumerate(sts)]
        outs = [dot(probs[p], part(w, 2048 + p * 128), TN) for p in range(8)]
        for p, o in enumerate(outs):
            o = jnp.where(first, o[:64], o[64:]).astype(bf)
            at = slice(p * 128, p * 128 + 128)
            att[w * 32 : w * 32 + 32, at] = o[:32]
            if w < 7:
                att_b[w * 32 : w * 32 + 32, at] = o[32:]
            else:
                att[256:288, at] = o[32:]
    m = dot(att[...], pw[...]) + xr[...]
    for k in range(4):
        mixed[k] = jnp.concatenate([m[w * 32 + k * 8 : w * 32 + k * 8 + 8] for w in range(8)], axis=0).astype(bf)
        corner[k] = m[224 + k * 8 : 232 + k * 8].astype(bf)
        mixed_side[k] = m[224 + k * 8 : 232 + k * 8].astype(bf)
        mixed_side[4 + k] = m[256 + k * 8 : 264 + k * 8].astype(bf)


def attend(shift, scale, own, rows, side, diag, tail, xr_b, qkv_b, bias, qw, pw):
    return call(
        attend_body, "window_attention", [((4, 64, 1024), bf), ((8, 8, 1024), bf), ((4, 8, 1024), bf), ((224, 1024), bf)],
        [pltpu.VMEM((288, 1024), f32), pltpu.VMEM((288, 1024), bf), pltpu.VMEM((288, 3072), bf),
         pltpu.VMEM((288, 1024), bf), pltpu.VMEM((256, 256), bf)],
        30, 3_500_000_000, 14_000_000, (shift, scale), (),
        (own, rows, side, diag, tail, xr_b, qkv_b, bias, qw, pw))


def interleaved(buf, slot, conv_rows, sp, b0, n):
    for q in range(2):
        o = conv_rows[q] + sp[:, (2 * q + b0) * 384 : (2 * q + b0) * 384 + 384]
        for m, part in enumerate(thirds(o)):
            buf[slot, m, pl.ds(q, n, stride=2)] = part
    return jnp.concatenate([buf[slot, m, 0 : 2 * n] for m in range(3)], axis=1).astype(bf)


def kept_out_body(shift, att, xr, side, conv, pw, uw, out, head, xs, buf):
    _, _, base, _ = halves(shift)
    c = shift[1]
    m = dot(att[...], pw[...]) + xr[...].reshape(224, 1024).astype(f32)
    for k in range(4):
        row = jnp.concatenate([m[w * 32 + k * 8 : w * 32 + k * 8 + 8] for w in range(7)] + [side[4 + k].astype(f32)], axis=0)
        head[k] = row[:8].astype(bf)
        xs[k] = pltpu.roll(row, c, axis=0).astype(bf)
    for g in range(2):
        sp = dot(xs[2 * g : 2 * g + 2].reshape(128, 1024), uw[...])
        for i in range(2):
            k = 2 * g + i
            for p in range(2):
                r = 2 * (4 - base + k) + p
                cr = [conv[r, q].astype(f32) for q in range(2)]
                out[2 * k + p] = interleaved(buf, (2 * k + p) % 4, cr, sp[i * 64 : i * 64 + 64], p, 64)


def kept_out(shift, att, xr, side, conv, pw, uw):
    return call(
        kept_out_body, "kept_out", [((8, 128, 384), bf), ((4, 8, 1024), bf)],
        [pltpu.VMEM((4, 64, 1024), bf), pltpu.VMEM((4, 3, 136, 128), f32)],
        20, 1_300_000_000, 8_000_000, (shift,), (), (att, xr, side, conv, pw, uw))


def moved_out_body(shift, own, rows, left, diag, head, res, conv, uw, out, xs, buf):
    _, up, base, received = halves(shift)
    c = shift[1]
    for k in range(4):
        got = received(k)
        row = jnp.concatenate(
            [jnp.where(got, diag[k], left[k]).astype(f32),
             jnp.where(got, rows[k], own[k]).astype(f32)], axis=0)
        xs[k * 64 : k * 64 + 64] = pltpu.roll(row, 64 + c, axis=0)[:64].astype(bf)
    ends = [
        pltpu.roll(jnp.concatenate([left[4 + k].astype(f32), head[k].astype(f32)], axis=0), 8 + c, axis=0)[:8]
        for k in range(4)
    ]
    xs[256:288] = jnp.concatenate(ends, axis=0).astype(bf)
    sp = dot(xs[...], uw[...])
    for k in range(4):
        for p in range(2):
            r = 2 * (base + k) + p
            cr = [conv[r, q].astype(f32) for q in range(2)]
            out[r] = interleaved(buf, (2 * k + p) % 4, cr, sp[k * 64 : k * 64 + 64], p, 64)
    for k in range(4):
        for p in range(2):
            r = 2 * (4 - base + k) + p
            cr = [conv[r, q, 0:16].astype(f32)[:8] for q in range(2)]
            out[r] = res[2 * k + p]
            out[r, 0:16] = interleaved(buf, (2 * k + p) % 4, cr, sp[256 + k * 8 : 264 + k * 8], p, 8)


def moved_out(shift, own, rows, left, diag, head, res, conv, uw):
    return call(
        moved_out_body, "moved_out", [((16, 128, 384), bf)],
        [pltpu.VMEM((288, 1024), bf), pltpu.VMEM((4, 3, 136, 128), f32)],
        24, 1_000_000_000, 9_000_000, (shift,), (), (own, rows, left, diag, head, res, conv, uw))[0]


def send(value, lat_step, lon_step):
    lats, lons = lax.axis_size("lat"), lax.axis_size("lon")
    pairs = [
        (a * lons + b, ((a + lat_step) % lats) * lons + (b + lon_step) % lons)
        for a in range(lats)
        for b in range(lons)
    ]
    return lax.ppermute(value, ("lat", "lon"), pairs)


def on_device(fine, conv_weight, merge_weight, qkv_weight, proj_weight, up_weight, logit_scale, pos_bias, shift):
    lat = lax.axis_index("lat").astype(jnp.int32).reshape(1)
    top = send(fine[15:16], 1, 0)
    bot = send(fine[0:1], -1, 0)
    bias = bias_table(shift, lat, pos_bias)
    left = send(jnp.concatenate([top[:, 127], fine[:, 127], bot[:, 127]], axis=0), 0, 1)
    right = send(jnp.concatenate([top[:, 0], fine[:, 0], bot[:, 0]], axis=0), 0, -1)
    cw, mw, qw, pw, uw = conv_weight.reshape(3456, 384), merge_weight, qkv_weight, proj_weight, up_weight
    conv, edge = conv_main(lat, fine, cw, top, bot)
    conv, moved, side, corner = merge_moved(shift, lat, conv, edge, left, right, cw, mw)
    up = shift[0] <= 4

    def ahead(step):
        def branch(moved, side, corner, conv, mw, qw):
            got = send(moved, step, 0), send(side, 0, -1), send(corner, step, -1)
            return got + tuple(kept(shift, conv, mw, qw))

        return branch

    def behind(step):
        def branch(mixed, side, corner, att_b, xr_b, conv, pw, uw):
            got = send(mixed, step, 0), send(side, 0, 1), send(corner, step, 1)
            return got + tuple(kept_out(shift, att_b, xr_b, side, conv, pw, uw))

        return branch

    rows, side, diag, tail, xr_b, qkv_b = lax.cond(up, ahead(-1), ahead(1), moved, side, corner, conv, mw, qw)
    mixed, mixed_side, corner, att_b = attend(
        shift, logit_scale, moved, rows, side, diag, tail, xr_b, qkv_b, bias, qw, pw)
    rows, side, diag, res, head = lax.cond(up, behind(1), behind(-1), mixed, mixed_side, corner, att_b, xr_b, conv, pw, uw)
    return moved_out(shift, mixed, rows, side, diag, head, res, conv, uw)


def solution(mesh):
    return jax.shard_map(
        on_device,
        mesh=mesh,
        in_specs=(P("lat", "lon", None), P(), P(), P(), P(), P(), P(), P(), P()),
        out_specs=P("lat", "lon", None),
        check_vma=False,
    )
```
